128 devices in a mesh: sect: 16 (over x, z), rup: 8 (over y, core).
Axes of the slice: x: 4, y: 4, z: 4, core: 2. Of those that a mesh axis runs over, the one named last changes fastest.
Arguments:
- green_tensor: bfloat16 [64, 2, 6, 3, 1024, 128], P('sect', None, None, None, 'rup'), may hold values from -6 to 6
- slip_rate: bfloat16 [64, 32, 2, 1024, 128], P('rup', 'sect'), may hold values from -6 to 6
- moment_tensor: bfloat16 [64, 32, 6, 128], P('rup', 'sect'), may hold values from -0.02734375 to 0.02734375
- section_ids: int32 [64, 32], P('rup', 'sect'), may hold values from 0 to 15, as said below
- block_ids: int32 [64, 32], P('rup', 'sect'), may hold values from 0 to 3
Outputs:
- seismogram: float32 [64, 3, 2048], P('sect', None, 'rup')
The draws below stay inside these ranges and needn't reach their ends.
Inputs may be any that keep to these rules, and one draw needn't show every extreme that they name: `section_ids`: among the 16 entries held by one device (one block of 8 ruptures times one block of 2 list positions), no section is named more than 2 times, and one section, the same for every device, is named exactly 2 times by every device.
All inputs are finite; a program needn't handle non-finite values.
Results may differ from the reference program's by a relative error of at most 0.0029.
Values may be sent and summed in bfloat16 or wider, within the bound.
No kernel may reach another device: no remote copies, remote signals or barrier semaphores. Data moves between devices by JAX's collectives and lax.ppermute only.
A program may use at most 128 MiB of HBM per device.

```python
import math
import jax
import jax.numpy as jnp
from jax import lax

F = 1024
PB = 128
BLK_SECT = 4
R_DEV = 8
LIST_DEV = 2
CAP = 2
R = 64
LIST = 32
NBLK = 64
NT = 2048
N_SECT = 16
N_RUP = 8


def draw_section_ids(key, part):
    entries = R_DEV * LIST_DEV
    devices = N_RUP * N_SECT
    hot_key, rest_key = jax.random.split(jax.random.fold_in(key, 11))
    hottest = jax.random.randint(hot_key, (), 0, N_SECT)
    others = jnp.arange(N_SECT - 1, dtype=jnp.int32)
    others = others + (others >= hottest).astype(jnp.int32)
    spare_ids = jnp.repeat(others, CAP)

    def one_device(device_key):
        first_key, second_key = jax.random.split(device_key)
        picked = jax.random.permutation(first_key, spare_ids)[:entries - CAP]
        filled = jnp.concatenate([jnp.full((CAP,), hottest, jnp.int32), picked])
        return jax.random.permutation(second_key, filled)
    device_keys = jax.random.split(rest_key, devices)
    assigned = jax.vmap(one_device)(device_keys)
    assigned = assigned.reshape(N_RUP, N_SECT, R_DEV, LIST_DEV)
    assigned = jnp.transpose(assigned, (0, 2, 1, 3))
    return assigned.reshape(R_DEV * N_RUP, LIST_DEV * N_SECT).astype(jnp.int32)


def plant(values, own_key, low, largest):
    place = [jax.random.randint(jax.random.fold_in(own_key, axis), (), 0, length) for axis, length in enumerate(values.shape)]
    longest = values.shape.index(max(values.shape))
    neighbour = place[:longest] + [(place[longest] + 1) % values.shape[longest]] + place[longest + 1:]
    return values.at[tuple(place)].set(low).at[tuple(neighbour)].set(largest)


def level_of(key, extent, cuts, low, top_value):
    def one(dim, parts):
        draws = jax.random.uniform(jax.random.fold_in(jax.random.fold_in(key, 6), dim), (parts,), jnp.float32, low / len(cuts), top_value / len(cuts))
        return jnp.repeat(jnp.exp(draws), extent[dim] // parts).reshape((-1,) + (1,) * (len(extent) - dim - 1))

    gain = one(*cuts[0])
    for cut in cuts[1:]:
        gain = gain * one(*cut)
    return gain


def gaussian(own_key, dims, spread, bound, pieces=(), kind=jnp.bfloat16):
    values = jax.random.normal(own_key, dims, jnp.float32) * spread
    if len(pieces) > 0:
        values = level_of(own_key, dims, pieces, -0.22, 0.18) * values
    return jnp.clip(values, min=-bound, max=bound).astype(kind)


def setup_inputs(seed: int = 0) -> dict:
    seeds = jax.random.split(jax.random.key(seed), 6)
    return {
        "green_tensor": gaussian(seeds[0], (NBLK, 2, 6, 3, F, PB), 1.0, 6.0, ((0, 16), (4, 8))),
        "slip_rate": gaussian(seeds[1], (R, LIST, 2, F, PB), 1.0, 6.0, ((0, 8), (1, 16))),
        "moment_tensor": gaussian(seeds[2], (R, LIST, 6, PB), (12 * PB * LIST) ** -0.5, 0.02734375, ((0, 8), (1, 16))),
        "section_ids": draw_section_ids(jax.random.fold_in(seeds[5], 71), 0),
        "block_ids": plant(jax.random.randint(seeds[4], (R, LIST), 0, BLK_SECT), jax.random.fold_in(seeds[4], 1), 0, BLK_SECT - 1).astype(jnp.int32),
    }


def phase_table(freq_ids, time_ids, samples):
    phases = freq_ids[:, None] * time_ids[None, :] % samples
    angles = phases.astype(jnp.float32) * (2.0 * math.pi / samples)
    return (jnp.cos(angles), jnp.sin(angles))

def reference(green_tensor, slip_rate, moment_tensor, section_ids, block_ids):
    tensor_ids = (section_ids * BLK_SECT + block_ids).astype(jnp.int32)

    def one_rupture(inputs):
        rupture_slip, rupture_moment, rupture_ids = inputs
        weighted = (rupture_moment[:, None, :, None, :].astype(jnp.float32) * rupture_slip[:, :, None, :, :].astype(jnp.float32)).astype(jnp.bfloat16)
        weighted = lax.optimization_barrier(weighted).astype(jnp.float32)
        chosen = green_tensor[rupture_ids].astype(jnp.float32)
        products = jnp.einsum('lscfp,lgcjfp->sgjf', weighted, chosen, precision=lax.Precision.HIGHEST)
        real_part = products[0, 0] - products[1, 1]
        imag_part = products[0, 1] + products[1, 0]
        return jnp.stack([real_part, imag_part])
    spectra = lax.map(one_rupture, (slip_rate, moment_tensor, tensor_ids))
    cosine_table, sine_table = phase_table(jnp.arange(F, dtype=jnp.int32), jnp.arange(NT, dtype=jnp.int32), NT)
    seismogram = jnp.einsum('rjf,ft->rjt', spectra[:, 0], cosine_table, precision=lax.Precision.HIGHEST)
    seismogram = seismogram - jnp.einsum('rjf,ft->rjt', spectra[:, 1], sine_table, precision=lax.Precision.HIGHEST)
    return seismogram / math.sqrt(F)
```

```python
import functools
import math

import jax
import jax.numpy as jnp
import numpy as np
from jax import lax
from jax.experimental import pallas as pl
from jax.experimental.pallas import tpu as pltpu
from jax.sharding import PartitionSpec as P

PARTS = (6, 2)
STEP = 16
LANES = 128


def phase_table(freq_ids, time_ids, samples):
    phases = freq_ids[:, None] * time_ids[None, :] % samples
    angles = phases.astype(jnp.float32) * (2.0 * math.pi / samples)
    return (jnp.cos(angles), jnp.sin(angles))


def split_kernel(slip_ref, *out_refs):
    lists, parts, devices = slip_ref.shape[1:4]
    for part in range(parts):
        for d in range(devices):
            turned = [
                jnp.swapaxes(slip_ref[:, l, part, d].astype(jnp.float32), 0, 1) for l in range(lists)
            ]
            turned = jnp.concatenate(turned, axis=1).astype(slip_ref.dtype)
            first = 0
            for out_ref in out_refs:
                count = out_ref.shape[2]
                out_ref[d, 0, :, part] = turned[first : first + count]
                first += count


def split(slip, counts, sects, some):
    rows, lists, parts, devices, sub, points = slip.shape
    steps = sects // some
    shapes = [(sects, devices // sects, count, parts, lists * rows, points) for count in counts]
    return pl.pallas_call(
        split_kernel,
        grid=(devices // sects, steps),
        in_specs=[
            pl.BlockSpec((rows, lists, parts, some, sub, points), lambda k, i: (0, 0, 0, k * steps + i, 0, 0))
        ],
        out_specs=[pl.BlockSpec((some, 1) + shape[2:], lambda k, i: (i, k, 0, 0, 0, 0)) for shape in shapes],
        out_shape=[jax.ShapeDtypeStruct(shape, slip.dtype) for shape in shapes],
        compiler_params=pltpu.CompilerParams(vmem_limit_bytes=60 * 2**20),
    )(slip)


def contract_kernel(width, blocks, sub, first, final, *refs):
    if final:
        slip_ref, moment_ref, green_ref, fold_ref, prev_ref, out_ref, acc_ref, sum_ref = refs
    else:
        slip_ref, moment_ref, green_ref, fold_ref, sum_ref, acc_ref = refs
    rups, sects, rows_per = moment_ref.shape[:3]
    comps = rows_per - 1
    entries, points = moment_ref.shape[3:]
    half = entries // 2
    cols = green_ref.shape[2]
    green = jnp.concatenate([green_ref[0, c] for c in range(comps)], axis=1)
    col = lax.broadcasted_iota(jnp.int32, (1, 1, 1, cols), 3)
    col_block = (col // width * blocks + col % blocks).astype(jnp.float32)
    acc_ref[...] = jnp.zeros(acc_ref.shape, jnp.float32)
    f = pl.program_id(0)

    @pl.when(f == 0)
    def _():
        sum_ref[...] = prev_ref[...] if final else jnp.zeros(sum_ref.shape, jnp.float32)

    def step(i, carry):
        some = pl.ds(i * STEP, STEP)
        ids = moment_ref[:, some, comps].astype(jnp.float32)
        mask = jnp.concatenate([ids] * (cols // points), axis=3) == col_block
        for part in range(2):
            slip = jnp.swapaxes(slip_ref[some, :, 0, part], 0, 1)
            weighted = jnp.concatenate(
                [
                    (slip * moment_ref[:, some, c]).reshape(rups * STEP * entries, points)
                    for c in range(comps)
                ],
                axis=1,
            )
            products = lax.dot_general(
                weighted, green, (((1,), (1,)), ((), ())), preferred_element_type=jnp.float32
            )
            kept = jnp.where(mask, products.reshape(rups, STEP, entries, cols), 0.0)
            kept = kept.reshape(rups, STEP, 2, half, cols)
            total = kept[:, 0, 0] + kept[:, 0, 1]
            for g in range(1, STEP):
                total = total + kept[:, g, 0] + kept[:, g, 1]
            acc_ref[part] += total
        return carry

    lax.fori_loop(0, sects // STEP, step, 0)
    spectrum = None
    for part in range(2):
        rest = acc_ref[part].reshape(rups * half, cols)
        for _ in range(3):
            piece = rest.astype(jnp.bfloat16)
            term = jnp.dot(piece, fold_ref[part], preferred_element_type=jnp.float32)
            spectrum = term if spectrum is None else spectrum + term
            rest = rest - piece.astype(jnp.float32)
    sum_ref[...] += pltpu.roll(spectrum, f + first, 1)
    if final:

        @pl.when(f == pl.num_programs(0) - 1)
        def _():
            owned = out_ref.shape[1]
            for s in range(sects):
                mine = sum_ref[s * owned : (s + 1) * owned]
                for k in range(rups):
                    out_ref[s * rups + k] = mine


def contract(slip, moment, green, fold, prev, first, width, blocks):
    sects, rups, freqs, _, entries, points = slip.shape
    sub = green.shape[0]
    cols = green.shape[2]
    ruptures = rups * entries // 2
    comps = moment.shape[2] - 1
    final = prev is not None
    in_specs = [
        pl.BlockSpec((sects, rups, 1, 2, entries, points), lambda f: (0, 0, f, 0, 0, 0)),
        pl.BlockSpec(moment.shape, lambda f: (0, 0, 0, 0, 0)),
        pl.BlockSpec((1,) + green.shape[1:], lambda f: (f + first, 0, 0, 0)),
        pl.BlockSpec(fold.shape, lambda f: (0, 0, 0)),
    ]
    args = [slip, moment, green, fold]
    scratch = [pltpu.VMEM((2, rups, entries // 2, cols), jnp.float32)]
    if final:
        in_specs.append(pl.BlockSpec(prev.shape, lambda f: (0, 0)))
        args.append(prev)
        shape = (sects * rups, ruptures // sects, LANES)
        scratch.append(pltpu.VMEM((ruptures, LANES), jnp.float32))
    else:
        shape = (ruptures, LANES)
    return pl.pallas_call(
        functools.partial(contract_kernel, width, blocks, sub, first, final),
        grid=(freqs,),
        in_specs=in_specs,
        out_specs=pl.BlockSpec(shape, lambda f: (0,) * len(shape)),
        out_shape=jax.ShapeDtypeStruct(shape, jnp.float32),
        scratch_shapes=scratch,
        compiler_params=pltpu.CompilerParams(vmem_limit_bytes=60 * 2**20),
        cost_estimate=pl.CostEstimate(
            flops=freqs * 4 * sects * rups * entries * comps * points * cols,
            bytes_accessed=freqs * (sects * rups * entries * points * 4 + comps * cols * points * 2),
            transcendentals=0,
        ),
    )(*args)


def fold_table(cols, blocks, sub):
    col = np.arange(cols)
    part, direction = col // blocks % 2, col // (2 * blocks) % 3
    out = np.arange(LANES)
    value = np.where((out < 6 * sub) & (out % sub == 0), out // sub, -1)
    same = (direction[:, None] == (value % 3)[None, :]) & (value >= 0)[None, :]
    equal = part[:, None] == (value // 3)[None, :]
    sign = np.where(value // 3 == 0, -1.0, 1.0)[None, :]
    real_slip = np.where(same & equal, 1.0, 0.0)
    imag_slip = np.where(same & ~equal, sign, 0.0)
    return jnp.asarray(np.stack([real_slip, imag_slip]), jnp.bfloat16)


def transform_table(first_time, times, frequencies, sects, rups, sub):
    samples = 2 * frequencies
    time_ids = first_time + jnp.arange(times, dtype=jnp.int32)
    base = np.arange(sects)[:, None] * sub + np.arange(rups)[None, :] * (frequencies // rups)
    base_cos, base_sin = phase_table(jnp.asarray(base.reshape(-1), jnp.int32), time_ids, samples)
    rest_cos, rest_sin = phase_table(jnp.arange(sub, dtype=jnp.int32), time_ids, samples)
    base_cos, base_sin, rest_cos, rest_sin = lax.optimization_barrier((base_cos, base_sin, rest_cos, rest_sin))
    cosine = rest_cos[:, None] * base_cos[None] - rest_sin[:, None] * base_sin[None]
    sine = rest_sin[:, None] * base_cos[None] + rest_cos[:, None] * base_sin[None]
    table = jnp.stack([cosine, -sine]) * (1.0 / math.sqrt(frequencies))
    table = table.reshape(2 * frequencies, times)
    high = table.astype(jnp.bfloat16)
    return high, (table - high.astype(jnp.float32)).astype(jnp.bfloat16)


def transform_kernel(sub, spectra_ref, high_ref, low_ref, out_ref, turned_ref, left_ref):
    dirs, owned = out_ref.shape[:2]
    devices = spectra_ref.shape[0]
    used = 2 * dirs * sub
    rows = left_ref.shape[0]
    for r in range(owned):
        turned_ref[r] = spectra_ref[:, r, :].T[:used]
    left_ref[...] = jnp.zeros(left_ref.shape, jnp.float32)
    for part in range(2):
        for f in range(sub):
            place = pl.ds((part * sub + f) * devices, devices)
            for r in range(owned):
                for j in range(dirs):
                    row = (part * dirs + j) * sub + f
                    left_ref[pl.ds(j * owned + r, 1), place] = turned_ref[r, pl.ds(row, 1), :]
    left = left_ref[...]
    high = left.astype(jnp.bfloat16)
    low = (left - high.astype(jnp.float32)).astype(jnp.bfloat16)
    both = jnp.concatenate([high, low], axis=0)
    first = jnp.dot(both, high_ref[...], preferred_element_type=jnp.float32)
    second = jnp.dot(high, low_ref[...], preferred_element_type=jnp.float32)
    result = first[:rows] + (first[rows:] + second)
    for j in range(dirs):
        out_ref[j] = result[j * owned : (j + 1) * owned]


def transform(spectra, high, low, dirs, sub):
    devices, owned, lanes = spectra.shape
    depth, times = high.shape
    return pl.pallas_call(
        functools.partial(transform_kernel, sub),
        out_shape=jax.ShapeDtypeStruct((dirs, owned, times), jnp.float32),
        scratch_shapes=[
            pltpu.VMEM((owned, 2 * dirs * sub, devices), jnp.float32),
            pltpu.VMEM((16, depth), jnp.float32),
        ],
        compiler_params=pltpu.CompilerParams(vmem_limit_bytes=16 * 2**20),
    )(spectra, high, low)


def body(green_tensor, slip_rate, moment_tensor, section_ids, block_ids):
    sects = lax.axis_size("sect")
    rups = lax.axis_size("rup")
    both = ("sect", "rup")
    blocks, _, comps, dirs, freq_slice, points = green_tensor.shape
    rup_rows, list_cols = section_ids.shape
    entries = rup_rows * list_cols
    frequencies = slip_rate.shape[3]
    sub = freq_slice // sects
    width = 2 * dirs * blocks
    cols = sects * width

    ids = (section_ids * blocks + block_ids).astype(jnp.bfloat16)
    ids = jnp.broadcast_to(ids.T.reshape(1, entries, 1), (1, entries, points))
    moment = jnp.transpose(moment_tensor, (2, 1, 0, 3)).reshape(comps, entries, points)
    moment = jnp.concatenate([moment, ids])
    moment = jnp.broadcast_to(moment[None], (sects,) + moment.shape)
    moment, green_tensor, slip_rate = lax.optimization_barrier((moment, green_tensor, slip_rate))
    moment = lax.all_to_all(moment, "sect", split_axis=0, concat_axis=0, tiled=True)

    green = green_tensor.reshape(blocks, 2, comps, dirs, sects, sub, points)
    green = jnp.transpose(green, (4, 5, 2, 3, 1, 0, 6)).reshape(sects, sub, comps, width, points)
    parts = split(slip_rate.reshape(rup_rows, list_cols, 2, rups * sects, sub, points), PARTS, sects, 8)
    green, moment, *parts = lax.optimization_barrier((green, moment, *parts))
    moment = lax.all_gather(moment, "rup", axis=0)
    green = lax.all_to_all(green, "sect", split_axis=0, concat_axis=0, tiled=True)
    green = jnp.transpose(green, (1, 2, 0, 3, 4)).reshape(sub, comps, cols, points)

    fold = fold_table(cols, blocks, sub)
    first_time = lax.axis_index("rup") * (2 * frequencies // rups)
    spectrum = None
    first = 0
    before = green
    for i, part in enumerate(parts):
        if i == 0:
            part, before, moment = lax.optimization_barrier((part, before, moment))
        else:
            part, before = lax.optimization_barrier((part, before))
        arrived = part.reshape((sects * rups,) + part.shape[2:])
        arrived = lax.all_to_all(arrived, both, split_axis=0, concat_axis=0, tiled=True)
        if i == 0:
            green = before
        else:
            spectrum = contract(before, moment, green, fold, spectrum, done, width, blocks)
        done = first
        before = arrived.reshape(part.shape)
        first += part.shape[2]
    first_time, before = lax.optimization_barrier((first_time, before))
    send = contract(before, moment, green, fold, spectrum, done, width, blocks)
    high, low = transform_table(first_time, 2 * frequencies // rups, frequencies, sects, rups, sub)

    all_freqs = lax.all_to_all(send, both, split_axis=0, concat_axis=0, tiled=True)
    return jnp.swapaxes(transform(all_freqs, high, low, dirs, sub), 0, 1)


def solution(mesh):
    placed = (
        P("sect", None, None, None, "rup", None),
        P("rup", "sect", None, None, None),
        P("rup", "sect", None, None),
        P("rup", "sect"),
        P("rup", "sect"),
    )
    return jax.shard_map(
        body, mesh=mesh, in_specs=placed, out_specs=P("sect", None, "rup"), check_vma=False
    )
```

```python
import functools
import math

import jax
import jax.numpy as jnp
import numpy as np
from jax import lax
from jax.experimental import pallas as pl
from jax.experimental.pallas import tpu as pltpu
from jax.sharding import PartitionSpec as P

PARTS = (6, 2)
STEP = 16
LANES = 128
PAD = 1


def phase_table(freq_ids, time_ids, samples):
    phases = freq_ids[:, None] * time_ids[None, :] % samples
    angles = phases.astype(jnp.float32) * (2.0 * math.pi / samples)
    return (jnp.cos(angles), jnp.sin(angles))


def load_rows(in_ref, wide_ref):
    rows = in_ref.shape[0]
    apart = wide_ref.shape[0] // rows
    for r in range(rows):
        block = in_ref[r].astype(jnp.float32).reshape(-1, in_ref.shape[-1])
        wide_ref[pl.ds(r * apart, block.shape[0])] = block
    return rows, apart


def split_slip_kernel(slip_ref, *refs):
    out_refs, wide_ref = refs[:-1], refs[-1]
    rows, apart = load_rows(slip_ref, wide_ref)
    lists, parts, devices, sub = slip_ref.shape[1:5]
    for part in range(parts):
        for d in range(devices):
            f = 0
            for out_ref in out_refs:
                for i in range(out_ref.shape[2]):
                    places = [((l * parts + part) * devices + d) * sub + f for l in range(lists)]
                    turned = [wide_ref[pl.ds(place, rows, stride=apart)] for place in places]
                    out_ref[d, 0, i, part] = jnp.concatenate(turned, axis=0).astype(slip_ref.dtype)
                    f += 1


def split_slip(slip, counts, sects):
    rows, lists, parts, devices, sub, points = slip.shape
    shapes = [(sects, devices // sects, count, parts, lists * rows, points) for count in counts]
    return pl.pallas_call(
        split_slip_kernel,
        grid=(devices // sects,),
        in_specs=[pl.BlockSpec((rows, lists, parts, sects, sub, points), lambda k: (0, 0, 0, k, 0, 0))],
        out_specs=[pl.BlockSpec((sects, 1) + shape[2:], lambda k: (0, k, 0, 0, 0, 0)) for shape in shapes],
        out_shape=[jax.ShapeDtypeStruct(shape, slip.dtype) for shape in shapes],
        scratch_shapes=[pltpu.VMEM((rows * (lists * parts * sects * sub + PAD), points), jnp.float32)],
        compiler_params=pltpu.CompilerParams(vmem_limit_bytes=60 * 2**20),
    )(slip)


def split_green_kernel(green_ref, out_ref, wide_ref):
    rows, apart = load_rows(green_ref, wide_ref)
    comps, dirs, sects, sub = green_ref.shape[1:5]
    for s in range(sects):
        for c in range(comps):
            for f in range(sub):
                places = [((c * dirs + j) * sects + s) * sub + f for j in range(dirs)]
                turned = [wide_ref[pl.ds(place, rows, stride=apart)] for place in places]
                out_ref[s, f, c] = jnp.concatenate(turned, axis=0).astype(green_ref.dtype)


def split_green(green, sects):
    rows, comps, dirs, _, sub, points = green.shape
    shape = (sects, sub, comps, dirs * rows, points)
    return pl.pallas_call(
        split_green_kernel,
        grid=(comps,),
        in_specs=[pl.BlockSpec((rows, 1, dirs, sects, sub, points), lambda c: (0, c, 0, 0, 0, 0))],
        out_specs=pl.BlockSpec((sects, sub, 1) + shape[3:], lambda c: (0, 0, c, 0, 0)),
        out_shape=jax.ShapeDtypeStruct(shape, green.dtype),
        scratch_shapes=[pltpu.VMEM((rows * (dirs * sects * sub + PAD), points), jnp.float32)],
        compiler_params=pltpu.CompilerParams(vmem_limit_bytes=60 * 2**20),
    )(green)


def contract_kernel(width, blocks, sub, first, final, *refs):
    if final:
        slip_ref, moment_ref, green_ref, fold_ref, prev_ref, out_ref, acc_ref, sum_ref = refs
    else:
        slip_ref, moment_ref, green_ref, fold_ref, sum_ref, acc_ref = refs
    rups, sects, rows_per = moment_ref.shape[:3]
    comps = rows_per - 1
    entries, points = moment_ref.shape[3:]
    half = entries // 2
    cols = sects * width
    green = jnp.concatenate([green_ref[:, 0, c].reshape(cols, points) for c in range(comps)], axis=1)
    col = lax.broadcasted_iota(jnp.int32, (1, 1, 1, cols), 3)
    col_block = (col // width * blocks + col % (2 * blocks) // 2).astype(jnp.float32)
    acc_ref[...] = jnp.zeros(acc_ref.shape, jnp.float32)
    f = pl.program_id(0)

    @pl.when(f == 0)
    def _():
        sum_ref[...] = prev_ref[...] if final else jnp.zeros(sum_ref.shape, jnp.float32)

    def step(i, carry):
        some = pl.ds(i * STEP, STEP)
        ids = moment_ref[:, some, comps].astype(jnp.float32)
        mask = jnp.concatenate([ids] * (cols // points), axis=3) == col_block
        for part in range(2):
            slip = jnp.swapaxes(slip_ref[some, :, 0, part], 0, 1)
            weighted = jnp.concatenate(
                [
                    (slip * moment_ref[:, some, c]).reshape(rups * STEP * entries, points)
                    for c in range(comps)
                ],
                axis=1,
            )
            products = lax.dot_general(
                weighted, green, (((1,), (1,)), ((), ())), preferred_element_type=jnp.float32
            )
            kept = jnp.where(mask, products.reshape(rups, STEP, entries, cols), 0.0)
            kept = kept.reshape(rups, STEP, 2, half, cols)
            total = kept[:, 0, 0] + kept[:, 0, 1]
            for g in range(1, STEP):
                total = total + kept[:, g, 0] + kept[:, g, 1]
            acc_ref[part] += total
        return carry

    lax.fori_loop(0, sects // STEP, step, 0)
    spectrum = None
    for part in range(2):
        rest = acc_ref[part].reshape(rups * half, cols)
        for _ in range(3):
            piece = rest.astype(jnp.bfloat16)
            term = jnp.dot(piece, fold_ref[part], preferred_element_type=jnp.float32)
            spectrum = term if spectrum is None else spectrum + term
            rest = rest - piece.astype(jnp.float32)
    sum_ref[...] += pltpu.roll(spectrum, f + first, 1)
    if final:

        @pl.when(f == pl.num_programs(0) - 1)
        def _():
            owned = out_ref.shape[1]
            for s in range(sects):
                mine = sum_ref[s * owned : (s + 1) * owned]
                for k in range(rups):
                    out_ref[s * rups + k] = mine


def contract(slip, moment, green, fold, prev, first, width, blocks):
    sects, rups, freqs, _, entries, points = slip.shape
    sub = green.shape[1]
    cols = sects * width
    ruptures = rups * entries // 2
    comps = moment.shape[2] - 1
    final = prev is not None
    in_specs = [
        pl.BlockSpec((sects, rups, 1, 2, entries, points), lambda f: (0, 0, f, 0, 0, 0)),
        pl.BlockSpec(moment.shape, lambda f: (0, 0, 0, 0, 0)),
        pl.BlockSpec((sects, 1) + green.shape[2:], lambda f: (0, f + first, 0, 0, 0)),
        pl.BlockSpec(fold.shape, lambda f: (0, 0, 0)),
    ]
    args = [slip, moment, green, fold]
    scratch = [pltpu.VMEM((2, rups, entries // 2, cols), jnp.float32)]
    if final:
        in_specs.append(pl.BlockSpec(prev.shape, lambda f: (0, 0)))
        args.append(prev)
        shape = (sects * rups, ruptures // sects, LANES)
        scratch.append(pltpu.VMEM((ruptures, LANES), jnp.float32))
    else:
        shape = (ruptures, LANES)
    return pl.pallas_call(
        functools.partial(contract_kernel, width, blocks, sub, first, final),
        grid=(freqs,),
        in_specs=in_specs,
        out_specs=pl.BlockSpec(shape, lambda f: (0,) * len(shape)),
        out_shape=jax.ShapeDtypeStruct(shape, jnp.float32),
        scratch_shapes=scratch,
        compiler_params=pltpu.CompilerParams(vmem_limit_bytes=60 * 2**20),
        cost_estimate=pl.CostEstimate(
            flops=freqs * 4 * sects * rups * entries * comps * points * cols,
            bytes_accessed=freqs * (sects * rups * entries * points * 4 + comps * cols * points * 2),
            transcendentals=0,
        ),
    )(*args)


def fold_table(cols, blocks, sub):
    col = np.arange(cols)
    part, direction = col % 2, col // (2 * blocks) % 3
    out = np.arange(LANES)
    value = np.where((out < 6 * sub) & (out % sub == 0), out // sub, -1)
    same = (direction[:, None] == (value % 3)[None, :]) & (value >= 0)[None, :]
    equal = part[:, None] == (value // 3)[None, :]
    sign = np.where(value // 3 == 0, -1.0, 1.0)[None, :]
    real_slip = np.where(same & equal, 1.0, 0.0)
    imag_slip = np.where(same & ~equal, sign, 0.0)
    return jnp.asarray(np.stack([real_slip, imag_slip]), jnp.bfloat16)


def transform_table(first_time, times, frequencies, sects, rups, sub):
    samples = 2 * frequencies
    time_ids = first_time + jnp.arange(times, dtype=jnp.int32)
    base = np.arange(sects)[:, None] * sub + np.arange(rups)[None, :] * (frequencies // rups)
    base_cos, base_sin = phase_table(jnp.asarray(base.reshape(-1), jnp.int32), time_ids, samples)
    rest_cos, rest_sin = phase_table(jnp.arange(sub, dtype=jnp.int32), time_ids, samples)
    base_cos, base_sin, rest_cos, rest_sin = lax.optimization_barrier((base_cos, base_sin, rest_cos, rest_sin))
    cosine = rest_cos[:, None] * base_cos[None] - rest_sin[:, None] * base_sin[None]
    sine = rest_sin[:, None] * base_cos[None] + rest_cos[:, None] * base_sin[None]
    table = jnp.stack([cosine, -sine]) * (1.0 / math.sqrt(frequencies))
    table = table.reshape(2 * frequencies, times)
    high = lax.reduce_precision(table, 8, 7)
    return high.astype(jnp.bfloat16), (table - high).astype(jnp.bfloat16)


def transform_kernel(sub, spectra_ref, high_ref, low_ref, out_ref, turned_ref, left_ref):
    dirs, owned = out_ref.shape[:2]
    devices = spectra_ref.shape[0]
    used = 2 * dirs * sub
    rows = left_ref.shape[0]
    for r in range(owned):
        turned_ref[r] = spectra_ref[:, r, :].T[:used]
    left_ref[...] = jnp.zeros(left_ref.shape, jnp.float32)
    for part in range(2):
        for f in range(sub):
            place = pl.ds((part * sub + f) * devices, devices)
            for r in range(owned):
                for j in range(dirs):
                    row = (part * dirs + j) * sub + f
                    left_ref[pl.ds(j * owned + r, 1), place] = turned_ref[r, pl.ds(row, 1), :]
    left = left_ref[...]
    high = left.astype(jnp.bfloat16)
    low = (left - high.astype(jnp.float32)).astype(jnp.bfloat16)
    both = jnp.concatenate([high, low], axis=0)
    first = jnp.dot(both, high_ref[...], preferred_element_type=jnp.float32)
    second = jnp.dot(high, low_ref[...], preferred_element_type=jnp.float32)
    result = first[:rows] + (first[rows:] + second)
    for j in range(dirs):
        out_ref[j] = result[j * owned : (j + 1) * owned]


def transform(spectra, high, low, dirs, sub):
    devices, owned, lanes = spectra.shape
    depth, times = high.shape
    return pl.pallas_call(
        functools.partial(transform_kernel, sub),
        out_shape=jax.ShapeDtypeStruct((dirs, owned, times), jnp.float32),
        scratch_shapes=[
            pltpu.VMEM((owned, 2 * dirs * sub, devices), jnp.float32),
            pltpu.VMEM((16, depth), jnp.float32),
        ],
        compiler_params=pltpu.CompilerParams(vmem_limit_bytes=16 * 2**20),
    )(spectra, high, low)


def body(green_tensor, slip_rate, moment_tensor, section_ids, block_ids):
    sects = lax.axis_size("sect")
    rups = lax.axis_size("rup")
    both = ("sect", "rup")
    blocks, _, comps, dirs, freq_slice, points = green_tensor.shape
    rup_rows, list_cols = section_ids.shape
    entries = rup_rows * list_cols
    frequencies = slip_rate.shape[3]
    sub = freq_slice // sects
    width = 2 * dirs * blocks
    cols = sects * width

    ids = (section_ids * blocks + block_ids).astype(jnp.bfloat16)
    ids = jnp.broadcast_to(ids.T.reshape(1, entries, 1), (1, entries, points))
    moment = jnp.transpose(moment_tensor, (2, 1, 0, 3)).reshape(comps, entries, points)
    moment = jnp.concatenate([moment, ids])
    moment = jnp.broadcast_to(moment[None], (sects,) + moment.shape)
    moment, green_tensor, slip_rate = lax.optimization_barrier((moment, green_tensor, slip_rate))
    moment = lax.all_to_all(moment, "sect", split_axis=0, concat_axis=0, tiled=True)

    green = split_green(green_tensor.reshape(blocks * 2, comps, dirs, sects, sub, points), sects)
    parts = split_slip(slip_rate.reshape(rup_rows, list_cols, 2, rups * sects, sub, points), PARTS, sects)
    green, moment, *parts = lax.optimization_barrier((green, moment, *parts))
    moment = lax.all_gather(moment, "rup", axis=0)
    green = lax.all_to_all(green, "sect", split_axis=0, concat_axis=0, tiled=True)

    fold = fold_table(cols, blocks, sub)
    first_time = lax.axis_index("rup") * (2 * frequencies // rups)
    spectrum = None
    first = 0
    before = green
    for i, part in enumerate(parts):
        if i == 0:
            part, before, moment = lax.optimization_barrier((part, before, moment))
        else:
            part, before = lax.optimization_barrier((part, before))
        arrived = part.reshape((sects * rups,) + part.shape[2:])
        arrived = lax.all_to_all(arrived, both, split_axis=0, concat_axis=0, tiled=True)
        if i == 0:
            green = before
        else:
            spectrum = contract(before, moment, green, fold, spectrum, done, width, blocks)
        done = first
        before = arrived.reshape(part.shape)
        first += part.shape[2]
    send = contract(before, moment, green, fold, spectrum, done, width, blocks)
    first_time, send = lax.optimization_barrier((first_time, send))
    high, low = transform_table(first_time, 2 * frequencies // rups, frequencies, sects, rups, sub)

    all_freqs = lax.all_to_all(send, both, split_axis=0, concat_axis=0, tiled=True)
    return jnp.swapaxes(transform(all_freqs, high, low, dirs, sub), 0, 1)


def solution(mesh):
    placed = (
        P("sect", None, None, None, "rup", None),
        P("rup", "sect", None, None, None),
        P("rup", "sect", None, None),
        P("rup", "sect"),
        P("rup", "sect"),
    )
    return jax.shard_map(
        body, mesh=mesh, in_specs=placed, out_specs=P("sect", None, "rup"), check_vma=False
    )
```

```python
import functools
import math

import jax
import jax.numpy as jnp
import numpy as np
from jax import lax
from jax.experimental import pallas as pl
from jax.experimental.pallas import tpu as pltpu
from jax.sharding import PartitionSpec as P

PARTS = (6, 2)
STEP = 16
LANES = 128
PAD = 1


def phase_table(freq_ids, time_ids, samples):
    phases = freq_ids[:, None] * time_ids[None, :] % samples
    angles = phases.astype(jnp.float32) * (2.0 * math.pi / samples)
    return (jnp.cos(angles), jnp.sin(angles))


def load_rows(block_ref, wide_ref):
    rows = block_ref.shape[0]
    apart = wide_ref.shape[0] // rows
    for r in range(rows):
        block = block_ref[r].astype(jnp.float32).reshape(-1, block_ref.shape[-1])
        wide_ref[pl.ds(r * apart, block.shape[0])] = block
    return rows, apart


def split_kernel(count, *refs):
    green_ref, slip_ref, green_out = refs[:3]
    slip_outs = refs[3 : 3 + count]
    green_in, slip_in, green_stage = refs[3 + count : 6 + count]
    slip_stages = refs[6 + count : 6 + 2 * count]
    green_wide, slip_wide, green_got, green_sent, slip_got, slip_sent = refs[6 + 2 * count :]
    comps, _, dirs, sects, sub, _ = green_in.shape
    rups, _, lists, parts = slip_in.shape[:4]

    def green_load(c):
        return pltpu.make_async_copy(green_ref.at[:, c], green_in.at[c], green_got.at[c])

    def slip_load(k):
        piece = slip_ref.at[:, :, :, pl.ds(k * sects, sects)]
        return pltpu.make_async_copy(piece, slip_in.at[k], slip_got.at[k])

    def green_store():
        return pltpu.make_async_copy(green_stage, green_out, green_sent)

    def slip_store(i, k):
        return pltpu.make_async_copy(slip_stages[i].at[:, k], slip_outs[i].at[:, k], slip_sent.at[i, k])

    for c in range(comps):
        green_load(c).start()
    for k in range(rups):
        slip_load(k).start()

    def green_step(c, carry):
        green_load(c).wait()
        rows, apart = load_rows(green_in.at[c], green_wide)
        for s in range(sects):
            for f in range(sub):
                places = [(j * sects + s) * sub + f for j in range(dirs)]
                turned = [green_wide[pl.ds(place, rows, stride=apart)] for place in places]
                green_stage[s, f, c] = jnp.concatenate(turned, axis=0).astype(green_stage.dtype)
        return carry

    lax.fori_loop(0, comps, green_step, 0)
    green_store().start()

    def slip_step(k, carry):
        slip_load(k).wait()
        rows, apart = load_rows(slip_in.at[k], slip_wide)
        for part in range(parts):
            for d in range(sects):
                f = 0
                for stage in slip_stages:
                    for i in range(stage.shape[2]):
                        places = [((l * parts + part) * sects + d) * sub + f for l in range(lists)]
                        turned = [slip_wide[pl.ds(place, rows, stride=apart)] for place in places]
                        stage[d, k, i, part] = jnp.concatenate(turned, axis=0).astype(stage.dtype)
                        f += 1
        for i in range(count):
            slip_store(i, k).start()
        return carry

    lax.fori_loop(0, rups, slip_step, 0)
    green_store().wait()
    for k in range(rups):
        for i in range(count):
            slip_store(i, k).wait()


def split(green, slip, counts):
    green_rows, comps, dirs, sects, sub, points = green.shape
    rows, lists, parts, devices = slip.shape[:4]
    rups = devices // sects
    green_shape = (sects, sub, comps, dirs * green_rows, points)
    slip_shapes = [(sects, rups, count, parts, lists * rows, points) for count in counts]
    kind = green.dtype
    anywhere = pl.BlockSpec(memory_space=pl.ANY)
    return pl.pallas_call(
        functools.partial(split_kernel, len(counts)),
        in_specs=[anywhere, anywhere],
        out_specs=[anywhere] * (1 + len(counts)),
        out_shape=[jax.ShapeDtypeStruct(shape, kind) for shape in [green_shape] + slip_shapes],
        scratch_shapes=[
            pltpu.VMEM((comps, green_rows, dirs, sects, sub, points), kind),
            pltpu.VMEM((rups, rows, lists, parts, sects, sub, points), kind),
            *[pltpu.VMEM(shape, kind) for shape in [green_shape] + slip_shapes],
            pltpu.VMEM((green_rows * (dirs * sects * sub + PAD), points), jnp.float32),
            pltpu.VMEM((rows * (lists * parts * sects * sub + PAD), points), jnp.float32),
            pltpu.SemaphoreType.DMA((comps,)),
            pltpu.SemaphoreType.DMA,
            pltpu.SemaphoreType.DMA((rups,)),
            pltpu.SemaphoreType.DMA((len(counts), rups)),
        ],
        compiler_params=pltpu.CompilerParams(vmem_limit_bytes=60 * 2**20),
        cost_estimate=pl.CostEstimate(
            flops=2 * (green.size + slip.size), bytes_accessed=4 * (green.size + slip.size), transcendentals=0
        ),
    )(green, slip)


def contract_kernel(width, blocks, sub, first, final, *refs):
    if final:
        slip_ref, moment_ref, green_ref, fold_ref, prev_ref, out_ref, acc_ref, sum_ref = refs
    else:
        slip_ref, moment_ref, green_ref, fold_ref, sum_ref, acc_ref = refs
    rups, sects, rows_per = moment_ref.shape[:3]
    comps = rows_per - 1
    entries, points = moment_ref.shape[3:]
    half = entries // 2
    cols = sects * width
    green = jnp.concatenate([green_ref[:, 0, c].reshape(cols, points) for c in range(comps)], axis=1)
    col = lax.broadcasted_iota(jnp.int32, (1, 1, 1, cols), 3)
    col_block = (col // width * blocks + col % (2 * blocks) // 2).astype(jnp.float32)
    acc_ref[...] = jnp.zeros(acc_ref.shape, jnp.float32)
    f = pl.program_id(0)

    @pl.when(f == 0)
    def _():
        sum_ref[...] = prev_ref[...] if final else jnp.zeros(sum_ref.shape, jnp.float32)

    def step(i, carry):
        some = pl.ds(i * STEP, STEP)
        ids = moment_ref[:, some, comps].astype(jnp.float32)
        mask = jnp.concatenate([ids] * (cols // points), axis=3) == col_block
        for part in range(2):
            slip = jnp.swapaxes(slip_ref[some, :, 0, part], 0, 1)
            weighted = jnp.concatenate(
                [
                    (slip * moment_ref[:, some, c]).reshape(rups * STEP * entries, points)
                    for c in range(comps)
                ],
                axis=1,
            )
            products = lax.dot_general(
                weighted, green, (((1,), (1,)), ((), ())), preferred_element_type=jnp.float32
            )
            kept = jnp.where(mask, products.reshape(rups, STEP, entries, cols), 0.0)
            kept = kept.reshape(rups, STEP, 2, half, cols)
            total = kept[:, 0, 0] + kept[:, 0, 1]
            for g in range(1, STEP):
                total = total + kept[:, g, 0] + kept[:, g, 1]
            acc_ref[part] += total
        return carry

    lax.fori_loop(0, sects // STEP, step, 0)
    spectrum = None
    for part in range(2):
        rest = acc_ref[part].reshape(rups * half, cols)
        for _ in range(3):
            piece = rest.astype(jnp.bfloat16)
            term = jnp.dot(piece, fold_ref[part], preferred_element_type=jnp.float32)
            spectrum = term if spectrum is None else spectrum + term
            rest = rest - piece.astype(jnp.float32)
    sum_ref[...] += pltpu.roll(spectrum, f + first, 1)
    if final:

        @pl.when(f == pl.num_programs(0) - 1)
        def _():
            owned = out_ref.shape[1]
            for s in range(sects):
                mine = sum_ref[s * owned : (s + 1) * owned]
                for k in range(rups):
                    out_ref[s * rups + k] = mine


def contract(slip, moment, green, fold, prev, first, width, blocks):
    sects, rups, freqs, _, entries, points = slip.shape
    sub = green.shape[1]
    cols = sects * width
    ruptures = rups * entries // 2
    comps = moment.shape[2] - 1
    final = prev is not None
    in_specs = [
        pl.BlockSpec((sects, rups, 1, 2, entries, points), lambda f: (0, 0, f, 0, 0, 0)),
        pl.BlockSpec(moment.shape, lambda f: (0, 0, 0, 0, 0)),
        pl.BlockSpec((sects, 1) + green.shape[2:], lambda f: (0, f + first, 0, 0, 0)),
        pl.BlockSpec(fold.shape, lambda f: (0, 0, 0)),
    ]
    args = [slip, moment, green, fold]
    scratch = [pltpu.VMEM((2, rups, entries // 2, cols), jnp.float32)]
    if final:
        in_specs.append(pl.BlockSpec(prev.shape, lambda f: (0, 0)))
        args.append(prev)
        shape = (sects * rups, ruptures // sects, LANES)
        scratch.append(pltpu.VMEM((ruptures, LANES), jnp.float32))
    else:
        shape = (ruptures, LANES)
    return pl.pallas_call(
        functools.partial(contract_kernel, width, blocks, sub, first, final),
        grid=(freqs,),
        in_specs=in_specs,
        out_specs=pl.BlockSpec(shape, lambda f: (0,) * len(shape)),
        out_shape=jax.ShapeDtypeStruct(shape, jnp.float32),
        scratch_shapes=scratch,
        compiler_params=pltpu.CompilerParams(vmem_limit_bytes=63_400_000),
        cost_estimate=pl.CostEstimate(
            flops=freqs * 4 * sects * rups * entries * comps * points * cols,
            bytes_accessed=freqs * (sects * rups * entries * points * 4 + comps * cols * points * 2),
            transcendentals=0,
        ),
    )(*args)


def fold_table(cols, blocks, sub):
    col = np.arange(cols)
    part, direction = col % 2, col // (2 * blocks) % 3
    out = np.arange(LANES)
    value = np.where((out < 6 * sub) & (out % sub == 0), out // sub, -1)
    same = (direction[:, None] == (value % 3)[None, :]) & (value >= 0)[None, :]
    equal = part[:, None] == (value // 3)[None, :]
    sign = np.where(value // 3 == 0, -1.0, 1.0)[None, :]
    real_slip = np.where(same & equal, 1.0, 0.0)
    imag_slip = np.where(same & ~equal, sign, 0.0)
    return jnp.asarray(np.stack([real_slip, imag_slip]), jnp.bfloat16)


def transform_table(first_time, times, frequencies, sects, rups, sub):
    samples = 2 * frequencies
    time_ids = first_time + jnp.arange(times, dtype=jnp.int32)
    base = np.arange(sects)[:, None] * sub + np.arange(rups)[None, :] * (frequencies // rups)
    base_cos, base_sin = phase_table(jnp.asarray(base.reshape(-1), jnp.int32), time_ids, samples)
    rest_cos, rest_sin = phase_table(jnp.arange(sub, dtype=jnp.int32), time_ids, samples)
    base_cos, base_sin, rest_cos, rest_sin = lax.optimization_barrier((base_cos, base_sin, rest_cos, rest_sin))
    cosine = rest_cos[:, None] * base_cos[None] - rest_sin[:, None] * base_sin[None]
    sine = rest_sin[:, None] * base_cos[None] + rest_cos[:, None] * base_sin[None]
    table = jnp.stack([cosine, -sine]) * (1.0 / math.sqrt(frequencies))
    table = table.reshape(2 * frequencies, times)
    high = lax.reduce_precision(table, 8, 7)
    return high.astype(jnp.bfloat16), (table - high).astype(jnp.bfloat16)


def transform_kernel(sub, spectra_ref, high_ref, low_ref, out_ref, turned_ref, left_ref):
    dirs, owned = out_ref.shape[:2]
    devices = spectra_ref.shape[0]
    used = 2 * dirs * sub
    rows = left_ref.shape[0]
    for r in range(owned):
        turned_ref[r] = spectra_ref[:, r, :].T[:used]
    left_ref[...] = jnp.zeros(left_ref.shape, jnp.float32)
    for part in range(2):
        for f in range(sub):
            place = pl.ds((part * sub + f) * devices, devices)
            for r in range(owned):
                for j in range(dirs):
                    row = (part * dirs + j) * sub + f
                    left_ref[pl.ds(j * owned + r, 1), place] = turned_ref[r, pl.ds(row, 1), :]
    left = left_ref[...]
    high = left.astype(jnp.bfloat16)
    low = (left - high.astype(jnp.float32)).astype(jnp.bfloat16)
    both = jnp.concatenate([high, low], axis=0)
    first = jnp.dot(both, high_ref[...], preferred_element_type=jnp.float32)
    second = jnp.dot(high, low_ref[...], preferred_element_type=jnp.float32)
    result = first[:rows] + (first[rows:] + second)
    for j in range(dirs):
        out_ref[j] = result[j * owned : (j + 1) * owned]


def transform(spectra, high, low, dirs, sub):
    devices, owned, lanes = spectra.shape
    depth, times = high.shape
    return pl.pallas_call(
        functools.partial(transform_kernel, sub),
        out_shape=jax.ShapeDtypeStruct((dirs, owned, times), jnp.float32),
        scratch_shapes=[
            pltpu.VMEM((owned, 2 * dirs * sub, devices), jnp.float32),
            pltpu.VMEM((16, depth), jnp.float32),
        ],
        compiler_params=pltpu.CompilerParams(vmem_limit_bytes=16 * 2**20),
    )(spectra, high, low)


def body(green_tensor, slip_rate, moment_tensor, section_ids, block_ids):
    sects = lax.axis_size("sect")
    rups = lax.axis_size("rup")
    both = ("sect", "rup")
    blocks, _, comps, dirs, freq_slice, points = green_tensor.shape
    rup_rows, list_cols = section_ids.shape
    entries = rup_rows * list_cols
    frequencies = slip_rate.shape[3]
    sub = freq_slice // sects
    width = 2 * dirs * blocks
    cols = sects * width

    ids = (section_ids * blocks + block_ids).astype(jnp.bfloat16)
    ids = jnp.broadcast_to(ids.T.reshape(1, entries, 1), (1, entries, points))
    moment = jnp.transpose(moment_tensor, (2, 1, 0, 3)).reshape(comps, entries, points)
    moment = jnp.concatenate([moment, ids])
    moment = jnp.broadcast_to(moment[None], (sects,) + moment.shape)
    moment, green_tensor, slip_rate = lax.optimization_barrier((moment, green_tensor, slip_rate))
    moment = lax.all_to_all(moment, "sect", split_axis=0, concat_axis=0, tiled=True)

    green, *parts = split(
        green_tensor.reshape(blocks * 2, comps, dirs, sects, sub, points),
        slip_rate.reshape(rup_rows, list_cols, 2, rups * sects, sub, points),
        PARTS,
    )
    green, moment, *parts = lax.optimization_barrier((green, moment, *parts))
    moment = lax.all_gather(moment, "rup", axis=0)
    green = lax.all_to_all(green, "sect", split_axis=0, concat_axis=0, tiled=True)

    fold = fold_table(cols, blocks, sub)
    first_time = lax.axis_index("rup") * (2 * frequencies // rups)
    spectrum = None
    first = 0
    before = green
    for i, part in enumerate(parts):
        if i == 0:
            part, before, moment = lax.optimization_barrier((part, before, moment))
        else:
            part, before = lax.optimization_barrier((part, before))
        arrived = part.reshape((sects * rups,) + part.shape[2:])
        arrived = lax.all_to_all(arrived, both, split_axis=0, concat_axis=0, tiled=True)
        if i == 0:
            green = before
        else:
            spectrum = contract(before, moment, green, fold, spectrum, done, width, blocks)
        done = first
        before = arrived.reshape(part.shape)
        first += part.shape[2]
    send = contract(before, moment, green, fold, spectrum, done, width, blocks)
    first_time, send = lax.optimization_barrier((first_time, send))
    high, low = transform_table(first_time, 2 * frequencies // rups, frequencies, sects, rups, sub)

    all_freqs = lax.all_to_all(send, both, split_axis=0, concat_axis=0, tiled=True)
    return jnp.swapaxes(transform(all_freqs, high, low, dirs, sub), 0, 1)


def solution(mesh):
    placed = (
        P("sect", None, None, None, "rup", None),
        P("rup", "sect", None, None, None),
        P("rup", "sect", None, None),
        P("rup", "sect"),
        P("rup", "sect"),
    )
    return jax.shard_map(
        body, mesh=mesh, in_specs=placed, out_specs=P("sect", None, "rup"), check_vma=False
    )
```

```python
import functools
import math

import jax
import jax.numpy as jnp
import numpy as np
from jax import lax
from jax.experimental import pallas as pl
from jax.experimental.pallas import tpu as pltpu
from jax.sharding import PartitionSpec as P

PARTS = (6, 2)
STEP = 16
LANES = 128
PAD = 1


def load_rows(block_ref, wide_ref):
    rows = block_ref.shape[0]
    apart = wide_ref.shape[0] // rows
    for r in range(rows):
        block = block_ref[r].astype(jnp.float32).reshape(-1, block_ref.shape[-1])
        wide_ref[pl.ds(r * apart, block.shape[0])] = block
    return rows, apart


def split_kernel(count, *refs):
    green_ref, slip_ref, green_out = refs[:3]
    slip_outs = refs[3 : 3 + count]
    green_in, slip_in, green_stage = refs[3 + count : 6 + count]
    slip_stages = refs[6 + count : 6 + 2 * count]
    green_wide, slip_wide, green_got, green_sent, slip_got, slip_sent = refs[6 + 2 * count :]
    comps, _, dirs, sects, sub, _ = green_in.shape
    rups, _, lists, parts = slip_in.shape[:4]

    def green_load(c):
        return pltpu.make_async_copy(green_ref.at[:, c], green_in.at[c], green_got.at[c])

    def slip_load(k):
        piece = slip_ref.at[:, :, :, pl.ds(k * sects, sects)]
        return pltpu.make_async_copy(piece, slip_in.at[k], slip_got.at[k])

    def green_store():
        return pltpu.make_async_copy(green_stage, green_out, green_sent)

    def slip_store(i, k):
        return pltpu.make_async_copy(slip_stages[i].at[:, k], slip_outs[i].at[:, k], slip_sent.at[i, k])

    for c in range(comps):
        green_load(c).start()
    for k in range(rups):
        slip_load(k).start()

    def green_step(c, carry):
        green_load(c).wait()
        rows, apart = load_rows(green_in.at[c], green_wide)
        for s in range(sects):
            for f in range(sub):
                places = [(j * sects + s) * sub + f for j in range(dirs)]
                turned = [green_wide[pl.ds(place, rows, stride=apart)] for place in places]
                green_stage[s, f, c] = jnp.concatenate(turned, axis=0).astype(green_stage.dtype)
        return carry

    lax.fori_loop(0, comps, green_step, 0)
    green_store().start()

    def slip_step(k, carry):
        slip_load(k).wait()
        rows, apart = load_rows(slip_in.at[k], slip_wide)
        for part in range(parts):
            for d in range(sects):
                f = 0
                for stage in slip_stages:
                    for i in range(stage.shape[2]):
                        places = [((l * parts + part) * sects + d) * sub + f for l in range(lists)]
                        turned = [slip_wide[pl.ds(place, rows, stride=apart)] for place in places]
                        stage[d, k, i, part] = jnp.concatenate(turned, axis=0).astype(stage.dtype)
                        f += 1
        for i in range(count):
            slip_store(i, k).start()
        return carry

    lax.fori_loop(0, rups, slip_step, 0)
    green_store().wait()
    for k in range(rups):
        for i in range(count):
            slip_store(i, k).wait()


def split(green, slip, counts):
    green_rows, comps, dirs, sects, sub, points = green.shape
    rows, lists, parts, devices = slip.shape[:4]
    rups = devices // sects
    green_shape = (sects, sub, comps, dirs * green_rows, points)
    slip_shapes = [(sects, rups, count, parts, lists * rows, points) for count in counts]
    kind = green.dtype
    anywhere = pl.BlockSpec(memory_space=pl.ANY)
    return pl.pallas_call(
        functools.partial(split_kernel, len(counts)),
        in_specs=[anywhere, anywhere],
        out_specs=[anywhere] * (1 + len(counts)),
        out_shape=[jax.ShapeDtypeStruct(shape, kind) for shape in [green_shape] + slip_shapes],
        scratch_shapes=[
            pltpu.VMEM((comps, green_rows, dirs, sects, sub, points), kind),
            pltpu.VMEM((rups, rows, lists, parts, sects, sub, points), kind),
            *[pltpu.VMEM(shape, kind) for shape in [green_shape] + slip_shapes],
            pltpu.VMEM((green_rows * (dirs * sects * sub + PAD), points), jnp.float32),
            pltpu.VMEM((rows * (lists * parts * sects * sub + PAD), points), jnp.float32),
            pltpu.SemaphoreType.DMA((comps,)),
            pltpu.SemaphoreType.DMA,
            pltpu.SemaphoreType.DMA((rups,)),
            pltpu.SemaphoreType.DMA((len(counts), rups)),
        ],
        compiler_params=pltpu.CompilerParams(vmem_limit_bytes=67_000_000),
        cost_estimate=pl.CostEstimate(
            flops=2 * (green.size + slip.size), bytes_accessed=4 * (green.size + slip.size), transcendentals=0
        ),
    )(green, slip)


def contract_kernel(width, blocks, sub, first, final, *refs):
    if final:
        slip_ref, moment_ref, green_ref, fold_ref, prev_ref, out_ref, acc_ref, sum_ref = refs
    else:
        slip_ref, moment_ref, green_ref, fold_ref, sum_ref, acc_ref = refs
    rups, sects, rows_per = moment_ref.shape[:3]
    comps = rows_per - 1
    entries, points = moment_ref.shape[3:]
    half = entries // 2
    cols = sects * width
    green = jnp.concatenate([green_ref[:, 0, c].reshape(cols, points) for c in range(comps)], axis=1)
    col = lax.broadcasted_iota(jnp.int32, (1, 1, 1, cols), 3)
    col_block = (col // width * blocks + col % (2 * blocks) // 2).astype(jnp.float32)
    acc_ref[...] = jnp.zeros(acc_ref.shape, jnp.float32)
    f = pl.program_id(0)

    @pl.when(f == 0)
    def _():
        sum_ref[...] = prev_ref[...] if final else jnp.zeros(sum_ref.shape, jnp.float32)

    def step(i, carry):
        some = pl.ds(i * STEP, STEP)
        ids = moment_ref[:, some, comps].astype(jnp.float32)
        mask = jnp.concatenate([ids] * (cols // points), axis=3) == col_block
        for part in range(2):
            slip = jnp.swapaxes(slip_ref[some, :, 0, part], 0, 1)
            weighted = jnp.concatenate(
                [
                    (slip * moment_ref[:, some, c]).reshape(rups * STEP * entries, points)
                    for c in range(comps)
                ],
                axis=1,
            )
            products = lax.dot_general(
                weighted, green, (((1,), (1,)), ((), ())), preferred_element_type=jnp.float32
            )
            kept = jnp.where(mask, products.reshape(rups, STEP, entries, cols), 0.0)
            kept = kept.reshape(rups, STEP, 2, half, cols)
            total = kept[:, 0, 0] + kept[:, 0, 1]
            for g in range(1, STEP):
                total = total + kept[:, g, 0] + kept[:, g, 1]
            acc_ref[part] += total
        return carry

    lax.fori_loop(0, sects // STEP, step, 0)
    spectrum = None
    for part in range(2):
        rest = acc_ref[part].reshape(rups * half, cols)
        for _ in range(3):
            piece = rest.astype(jnp.bfloat16)
            term = jnp.dot(piece, fold_ref[part], preferred_element_type=jnp.float32)
            spectrum = term if spectrum is None else spectrum + term
            rest = rest - piece.astype(jnp.float32)
    sum_ref[...] += pltpu.roll(spectrum, f + first, 1)
    if final:

        @pl.when(f == pl.num_programs(0) - 1)
        def _():
            owned = out_ref.shape[1]
            for s in range(sects):
                mine = sum_ref[s * owned : (s + 1) * owned]
                for k in range(rups):
                    out_ref[s * rups + k] = mine


def contract(slip, moment, green, fold, prev, first, width, blocks):
    sects, rups, freqs, _, entries, points = slip.shape
    sub = green.shape[1]
    cols = sects * width
    ruptures = rups * entries // 2
    comps = moment.shape[2] - 1
    final = prev is not None
    in_specs = [
        pl.BlockSpec((sects, rups, 1, 2, entries, points), lambda f: (0, 0, f, 0, 0, 0)),
        pl.BlockSpec(moment.shape, lambda f: (0, 0, 0, 0, 0)),
        pl.BlockSpec((sects, 1) + green.shape[2:], lambda f: (0, f + first, 0, 0, 0)),
        pl.BlockSpec(fold.shape, lambda f: (0, 0, 0)),
    ]
    args = [slip, moment, green, fold]
    scratch = [pltpu.VMEM((2, rups, entries // 2, cols), jnp.float32)]
    if final:
        in_specs.append(pl.BlockSpec(prev.shape, lambda f: (0, 0)))
        args.append(prev)
        shape = (sects * rups, ruptures // sects, LANES)
        scratch.append(pltpu.VMEM((ruptures, LANES), jnp.float32))
    else:
        shape = (ruptures, LANES)
    return pl.pallas_call(
        functools.partial(contract_kernel, width, blocks, sub, first, final),
        grid=(freqs,),
        in_specs=in_specs,
        out_specs=pl.BlockSpec(shape, lambda f: (0,) * len(shape)),
        out_shape=jax.ShapeDtypeStruct(shape, jnp.float32),
        scratch_shapes=scratch,
        compiler_params=pltpu.CompilerParams(vmem_limit_bytes=67_000_000),
        cost_estimate=pl.CostEstimate(
            flops=freqs * 4 * sects * rups * entries * comps * points * cols,
            bytes_accessed=freqs * (sects * rups * entries * points * 4 + comps * cols * points * 2),
            transcendentals=0,
        ),
    )(*args)


def fold_table(cols, blocks, sub):
    col = np.arange(cols)
    part, direction = col % 2, col // (2 * blocks) % 3
    out = np.arange(LANES)
    value = np.where((out < 6 * sub) & (out % sub == 0), out // sub, -1)
    same = (direction[:, None] == (value % 3)[None, :]) & (value >= 0)[None, :]
    equal = part[:, None] == (value // 3)[None, :]
    sign = np.where(value // 3 == 0, -1.0, 1.0)[None, :]
    real_slip = np.where(same & equal, 1.0, 0.0)
    imag_slip = np.where(same & ~equal, sign, 0.0)
    return jnp.asarray(np.stack([real_slip, imag_slip]), jnp.bfloat16)


def transform_table(rup, times, frequencies, sects, rups, sub):
    samples = 2 * frequencies
    unit = 2.0 * math.pi / samples
    base = np.arange(sects)[:, None] * sub + np.arange(rups)[None, :] * (frequencies // rups)
    base = base.reshape(-1, 1) * np.arange(times)[None, :] % samples * unit
    rest = np.arange(sub)[None, :, None] * np.arange(samples).reshape(rups, 1, times) % samples * unit
    scale = 1.0 / math.sqrt(frequencies)
    base_cos, base_sin = (jnp.asarray(f(base) * scale, jnp.float32) for f in (np.cos, np.sin))
    rest_cos, rest_sin = (
        lax.dynamic_index_in_dim(jnp.asarray(f(rest), jnp.float32), rup, 0, keepdims=False) for f in (np.cos, np.sin)
    )
    cosine = rest_cos[:, None] * base_cos[None] - rest_sin[:, None] * base_sin[None]
    sine = rest_sin[:, None] * base_cos[None] + rest_cos[:, None] * base_sin[None]
    table = jnp.stack([cosine, -sine]).reshape(2 * frequencies, times)
    high = lax.reduce_precision(table, 8, 7)
    return high.astype(jnp.bfloat16), (table - high).astype(jnp.bfloat16)


def transform_kernel(sub, spectra_ref, high_ref, low_ref, out_ref, turned_ref, left_ref):
    dirs, owned = out_ref.shape[:2]
    devices = spectra_ref.shape[0]
    used = 2 * dirs * sub
    rows = left_ref.shape[0]
    for r in range(owned):
        turned_ref[r] = spectra_ref[:, r, :].T[:used]
    left_ref[...] = jnp.zeros(left_ref.shape, jnp.float32)
    for part in range(2):
        for f in range(sub):
            place = pl.ds((part * sub + f) * devices, devices)
            for r in range(owned):
                for j in range(dirs):
                    row = (part * dirs + j) * sub + f
                    left_ref[pl.ds(j * owned + r, 1), place] = turned_ref[r, pl.ds(row, 1), :]
    left = left_ref[...]
    high = left.astype(jnp.bfloat16)
    low = (left - high.astype(jnp.float32)).astype(jnp.bfloat16)
    both = jnp.concatenate([high, low], axis=0)
    first = jnp.dot(both, high_ref[...], preferred_element_type=jnp.float32)
    second = jnp.dot(high, low_ref[...], preferred_element_type=jnp.float32)
    result = first[:rows] + (first[rows:] + second)
    for j in range(dirs):
        out_ref[j] = result[j * owned : (j + 1) * owned]


def transform(spectra, high, low, dirs, sub):
    devices, owned, lanes = spectra.shape
    depth, times = high.shape
    return pl.pallas_call(
        functools.partial(transform_kernel, sub),
        out_shape=jax.ShapeDtypeStruct((dirs, owned, times), jnp.float32),
        scratch_shapes=[
            pltpu.VMEM((owned, 2 * dirs * sub, devices), jnp.float32),
            pltpu.VMEM((16, depth), jnp.float32),
        ],
        compiler_params=pltpu.CompilerParams(vmem_limit_bytes=16 * 2**20),
    )(spectra, high, low)


def body(green_tensor, slip_rate, moment_tensor, section_ids, block_ids):
    sects = lax.axis_size("sect")
    rups = lax.axis_size("rup")
    both = ("sect", "rup")
    blocks, _, comps, dirs, freq_slice, points = green_tensor.shape
    rup_rows, list_cols = section_ids.shape
    entries = rup_rows * list_cols
    frequencies = slip_rate.shape[3]
    sub = freq_slice // sects
    width = 2 * dirs * blocks
    cols = sects * width

    ids = (section_ids * blocks + block_ids).astype(jnp.bfloat16)
    ids = jnp.broadcast_to(ids.T.reshape(1, entries, 1), (1, entries, points))
    moment = jnp.transpose(moment_tensor, (2, 1, 0, 3)).reshape(comps, entries, points)
    moment = jnp.concatenate([moment, ids])
    moment = jnp.broadcast_to(moment[None], (sects,) + moment.shape)
    moment, green_tensor, slip_rate = lax.optimization_barrier((moment, green_tensor, slip_rate))
    moment = lax.all_to_all(moment, "sect", split_axis=0, concat_axis=0, tiled=True)

    green, *parts = split(
        green_tensor.reshape(blocks * 2, comps, dirs, sects, sub, points),
        slip_rate.reshape(rup_rows, list_cols, 2, rups * sects, sub, points),
        PARTS,
    )
    green, moment, *parts = lax.optimization_barrier((green, moment, *parts))
    moment = lax.all_gather(moment, "rup", axis=0)
    green = lax.all_to_all(green, "sect", split_axis=0, concat_axis=0, tiled=True)

    fold = fold_table(cols, blocks, sub)
    rup = lax.axis_index("rup")
    spectrum = None
    first = 0
    before = green
    for i, part in enumerate(parts):
        if i == 0:
            part, before, moment = lax.optimization_barrier((part, before, moment))
        else:
            part, before = lax.optimization_barrier((part, before))
        arrived = part.reshape((sects * rups,) + part.shape[2:])
        arrived = lax.all_to_all(arrived, both, split_axis=0, concat_axis=0, tiled=True)
        if i == 0:
            green = before
        else:
            spectrum = contract(before, moment, green, fold, spectrum, done, width, blocks)
        done = first
        before = arrived.reshape(part.shape)
        first += part.shape[2]
    send = contract(before, moment, green, fold, spectrum, done, width, blocks)
    rup, send = lax.optimization_barrier((rup, send))
    high, low = transform_table(rup, 2 * frequencies // rups, frequencies, sects, rups, sub)

    all_freqs = lax.all_to_all(send, both, split_axis=0, concat_axis=0, tiled=True)
    return jnp.swapaxes(transform(all_freqs, high, low, dirs, sub), 0, 1)


def solution(mesh):
    placed = (
        P("sect", None, None, None, "rup", None),
        P("rup", "sect", None, None, None),
        P("rup", "sect", None, None),
        P("rup", "sect"),
        P("rup", "sect"),
    )
    return jax.shard_map(
        body, mesh=mesh, in_specs=placed, out_specs=P("sect", None, "rup"), check_vma=False
    )
```

```python
import functools
import math

import jax
import jax.numpy as jnp
import numpy as np
from jax import lax
from jax.experimental import pallas as pl
from jax.experimental.pallas import tpu as pltpu
from jax.sharding import PartitionSpec as P

PARTS = (6, 2)
LANES = 128
PAD = 1


def load_rows(block_ref, wide_ref):
    rows = block_ref.shape[0]
    apart = wide_ref.shape[0] // rows
    for r in range(rows):
        block = block_ref[r].astype(jnp.float32).reshape(-1, block_ref.shape[-1])
        wide_ref[pl.ds(r * apart, block.shape[0])] = block
    return rows, apart


def split_kernel(count, *refs):
    green_ref, slip_ref, green_out = refs[:3]
    slip_outs = refs[3 : 3 + count]
    green_in, slip_in, green_stage = refs[3 + count : 6 + count]
    slip_stages = refs[6 + count : 6 + 2 * count]
    green_wide, slip_wide, green_got, green_sent, slip_got, slip_sent = refs[6 + 2 * count :]
    comps, _, dirs, sects, sub, _ = green_in.shape
    rups, _, lists, parts = slip_in.shape[:4]

    def green_load(c):
        return pltpu.make_async_copy(green_ref.at[:, c], green_in.at[c], green_got.at[c])

    def slip_load(k):
        piece = slip_ref.at[:, :, :, pl.ds(k * sects, sects)]
        return pltpu.make_async_copy(piece, slip_in.at[k], slip_got.at[k])

    def green_store():
        return pltpu.make_async_copy(green_stage, green_out, green_sent)

    def slip_store(i, k):
        return pltpu.make_async_copy(slip_stages[i].at[:, k], slip_outs[i].at[:, k], slip_sent.at[i, k])

    for c in range(comps):
        green_load(c).start()
    for k in range(rups):
        slip_load(k).start()

    def green_step(c, carry):
        green_load(c).wait()
        rows, apart = load_rows(green_in.at[c], green_wide)
        for s in range(sects):
            for f in range(sub):
                places = [(j * sects + s) * sub + f for j in range(dirs)]
                turned = [green_wide[pl.ds(place, rows, stride=apart)] for place in places]
                green_stage[s, f, c] = jnp.concatenate(turned, axis=0).astype(green_stage.dtype)
        return carry

    lax.fori_loop(0, comps, green_step, 0)
    green_store().start()

    def slip_step(k, carry):
        slip_load(k).wait()
        rows, apart = load_rows(slip_in.at[k], slip_wide)
        for part in range(parts):
            for d in range(sects):
                f = 0
                for stage in slip_stages:
                    for i in range(stage.shape[2]):
                        places = [((l * parts + part) * sects + d) * sub + f for l in range(lists)]
                        turned = [slip_wide[pl.ds(place, rows, stride=apart)] for place in places]
                        stage[d, k, i, part] = jnp.concatenate(turned, axis=0).astype(stage.dtype)
                        f += 1
        for i in range(count):
            slip_store(i, k).start()
        return carry

    lax.fori_loop(0, rups, slip_step, 0)
    green_store().wait()
    for k in range(rups):
        for i in range(count):
            slip_store(i, k).wait()


def split(green, slip, counts):
    green_rows, comps, dirs, sects, sub, points = green.shape
    rows, lists, parts, devices = slip.shape[:4]
    rups = devices // sects
    green_shape = (sects, sub, comps, dirs * green_rows, points)
    slip_shapes = [(sects, rups, count, parts, lists * rows, points) for count in counts]
    kind = green.dtype
    anywhere = pl.BlockSpec(memory_space=pl.ANY)
    return pl.pallas_call(
        functools.partial(split_kernel, len(counts)),
        in_specs=[anywhere, anywhere],
        out_specs=[anywhere] * (1 + len(counts)),
        out_shape=[jax.ShapeDtypeStruct(shape, kind) for shape in [green_shape] + slip_shapes],
        scratch_shapes=[
            pltpu.VMEM((comps, green_rows, dirs, sects, sub, points), kind),
            pltpu.VMEM((rups, rows, lists, parts, sects, sub, points), kind),
            *[pltpu.VMEM(shape, kind) for shape in [green_shape] + slip_shapes],
            pltpu.VMEM((green_rows * (dirs * sects * sub + PAD), points), jnp.float32),
            pltpu.VMEM((rows * (lists * parts * sects * sub + PAD), points), jnp.float32),
            pltpu.SemaphoreType.DMA((comps,)),
            pltpu.SemaphoreType.DMA,
            pltpu.SemaphoreType.DMA((rups,)),
            pltpu.SemaphoreType.DMA((len(counts), rups)),
        ],
        compiler_params=pltpu.CompilerParams(vmem_limit_bytes=67_000_000),
        cost_estimate=pl.CostEstimate(
            flops=2 * (green.size + slip.size), bytes_accessed=4 * (green.size + slip.size), transcendentals=0
        ),
    )(green, slip)


def contract_kernel(width, blocks, sub, first, final, *refs):
    if final:
        slip_ref, moment_ref, green_ref, fold_ref, prev_ref, out_ref, sum_ref = refs
    else:
        slip_ref, moment_ref, green_ref, fold_ref, sum_ref = refs
    rups, sects, rows_per = moment_ref.shape[:3]
    comps = rows_per - 1
    entries, points = moment_ref.shape[3:]
    cols = sects * width
    green = jnp.concatenate([green_ref[:, 0, c].reshape(cols, points) for c in range(comps)], axis=1)
    row = lax.broadcasted_iota(jnp.int32, (cols, LANES), 0)
    row_block = (row // width * blocks + row % (2 * blocks) // 2).astype(jnp.float32)
    ids = moment_ref[0, :, comps].astype(jnp.float32)
    for k in range(1, rups):
        ids = ids + moment_ref[k, :, comps].astype(jnp.float32)
    f = pl.program_id(0)

    @pl.when(f == 0)
    def _():
        sum_ref[...] = prev_ref[...] if final else jnp.zeros(sum_ref.shape, jnp.float32)

    spectrum = None
    for part in range(2):
        slip = slip_ref[:, :, 0, part]
        weighted = jnp.concatenate(
            [
                (slip * jnp.swapaxes(moment_ref[:, :, c], 0, 1)).reshape(sects * LANES, points)
                for c in range(comps)
            ],
            axis=1,
        )
        products = lax.dot_general(green, weighted, (((1,), (1,)), ((), ())), preferred_element_type=jnp.float32)
        rest = None
        for s in range(sects):
            kept = jnp.where(row_block == ids[s, :1], products[:, s * LANES : (s + 1) * LANES], 0.0)
            rest = kept if rest is None else rest + kept
        for _ in range(3):
            piece = rest.astype(jnp.bfloat16)
            term = jnp.dot(fold_ref[part], piece, preferred_element_type=jnp.float32)
            spectrum = term if spectrum is None else spectrum + term
            rest = rest - piece.astype(jnp.float32)
    sum_ref[: spectrum.shape[0]] += pltpu.roll(spectrum, f + first, 0)
    if final:

        @pl.when(f == pl.num_programs(0) - 1)
        def _():
            owned = out_ref.shape[1]
            turned = sum_ref[...].T.reshape(rups, 2, entries // 2, LANES)
            turned = (turned[:, 0] + turned[:, 1]).reshape(rups * entries // 2, LANES)
            for s in range(sects):
                for k in range(rups):
                    out_ref[s * rups + k] = turned[s * owned : (s + 1) * owned]


def contract(slip, moment, green, fold, prev, first, width, blocks):
    sects, rups, freqs, _, entries, points = slip.shape
    sub = green.shape[1]
    cols = sects * width
    ruptures = rups * entries // 2
    comps = moment.shape[2] - 1
    final = prev is not None
    in_specs = [
        pl.BlockSpec((sects, rups, 1, 2, entries, points), lambda f: (0, 0, f, 0, 0, 0)),
        pl.BlockSpec(moment.shape, lambda f: (0, 0, 0, 0, 0)),
        pl.BlockSpec((sects, 1) + green.shape[2:], lambda f: (0, f + first, 0, 0, 0)),
        pl.BlockSpec(fold.shape, lambda f: (0, 0, 0)),
    ]
    args = [slip, moment, green, fold]
    scratch = []
    if final:
        in_specs.append(pl.BlockSpec(prev.shape, lambda f: (0, 0)))
        args.append(prev)
        shape = (sects * rups, ruptures // sects, LANES)
        scratch.append(pltpu.VMEM((LANES, LANES), jnp.float32))
    else:
        shape = (LANES, LANES)
    return pl.pallas_call(
        functools.partial(contract_kernel, width, blocks, sub, first, final),
        grid=(freqs,),
        in_specs=in_specs,
        out_specs=pl.BlockSpec(shape, lambda f: (0,) * len(shape)),
        out_shape=jax.ShapeDtypeStruct(shape, jnp.float32),
        scratch_shapes=scratch,
        compiler_params=pltpu.CompilerParams(vmem_limit_bytes=67_000_000),
        cost_estimate=pl.CostEstimate(
            flops=freqs * 4 * sects * rups * entries * comps * points * cols,
            bytes_accessed=freqs * (sects * rups * entries * points * 4 + comps * cols * points * 2),
            transcendentals=0,
        ),
    )(*args)


def fold_table(cols, blocks, sub):
    col = np.arange(cols)
    part, direction = col % 2, col // (2 * blocks) % 3
    out = np.arange(6 * sub)
    value = np.where(out % sub == 0, out // sub, -1)
    same = (direction[None, :] == (value % 3)[:, None]) & (value >= 0)[:, None]
    equal = part[None, :] == (value // 3)[:, None]
    sign = np.where(value // 3 == 0, -1.0, 1.0)[:, None]
    real_slip = np.where(same & equal, 1.0, 0.0)
    imag_slip = np.where(same & ~equal, sign, 0.0)
    return jnp.asarray(np.stack([real_slip, imag_slip]), jnp.bfloat16)


def transform_table(rup, times, frequencies, sects, rups, sub):
    samples = 2 * frequencies
    unit = 2.0 * math.pi / samples
    base = np.arange(sects)[:, None] * sub + np.arange(rups)[None, :] * (frequencies // rups)
    base = base.reshape(-1, 1) * np.arange(times)[None, :] % samples * unit
    rest = np.arange(sub)[None, :, None] * np.arange(samples).reshape(rups, 1, times) % samples * unit
    scale = 1.0 / math.sqrt(frequencies)
    base_cos, base_sin = (jnp.asarray(f(base) * scale, jnp.float32) for f in (np.cos, np.sin))
    rest_cos, rest_sin = (
        lax.dynamic_index_in_dim(jnp.asarray(f(rest), jnp.float32), rup, 0, keepdims=False) for f in (np.cos, np.sin)
    )
    cosine = rest_cos[:, None] * base_cos[None] - rest_sin[:, None] * base_sin[None]
    sine = rest_sin[:, None] * base_cos[None] + rest_cos[:, None] * base_sin[None]
    table = jnp.stack([cosine, -sine]).reshape(2 * frequencies, times)
    high = lax.reduce_precision(table, 8, 7)
    return high.astype(jnp.bfloat16), (table - high).astype(jnp.bfloat16)


def transform_kernel(sub, spectra_ref, high_ref, low_ref, out_ref, turned_ref, left_ref):
    dirs, owned = out_ref.shape[:2]
    devices = spectra_ref.shape[0]
    used = 2 * dirs * sub
    rows = left_ref.shape[0]
    for r in range(owned):
        turned_ref[r] = spectra_ref[:, r, :].T[:used]
    left_ref[...] = jnp.zeros(left_ref.shape, jnp.float32)
    for part in range(2):
        for f in range(sub):
            place = pl.ds((part * sub + f) * devices, devices)
            for r in range(owned):
                for j in range(dirs):
                    row = (part * dirs + j) * sub + f
                    left_ref[pl.ds(j * owned + r, 1), place] = turned_ref[r, pl.ds(row, 1), :]
    left = left_ref[...]
    high = left.astype(jnp.bfloat16)
    low = (left - high.astype(jnp.float32)).astype(jnp.bfloat16)
    both = jnp.concatenate([high, low], axis=0)
    first = jnp.dot(both, high_ref[...], preferred_element_type=jnp.float32)
    second = jnp.dot(high, low_ref[...], preferred_element_type=jnp.float32)
    result = first[:rows] + (first[rows:] + second)
    for j in range(dirs):
        out_ref[j] = result[j * owned : (j + 1) * owned]


def transform(spectra, high, low, dirs, sub):
    devices, owned, lanes = spectra.shape
    depth, times = high.shape
    return pl.pallas_call(
        functools.partial(transform_kernel, sub),
        out_shape=jax.ShapeDtypeStruct((dirs, owned, times), jnp.float32),
        scratch_shapes=[
            pltpu.VMEM((owned, 2 * dirs * sub, devices), jnp.float32),
            pltpu.VMEM((16, depth), jnp.float32),
        ],
        compiler_params=pltpu.CompilerParams(vmem_limit_bytes=16 * 2**20),
    )(spectra, high, low)


def body(green_tensor, slip_rate, moment_tensor, section_ids, block_ids):
    sects = lax.axis_size("sect")
    rups = lax.axis_size("rup")
    both = ("sect", "rup")
    blocks, _, comps, dirs, freq_slice, points = green_tensor.shape
    rup_rows, list_cols = section_ids.shape
    entries = rup_rows * list_cols
    frequencies = slip_rate.shape[3]
    sub = freq_slice // sects
    width = 2 * dirs * blocks
    cols = sects * width

    ids = jnp.tile((section_ids * blocks + block_ids).T.reshape(entries), rups)
    mine = jnp.arange(points, dtype=jnp.int32) // entries == lax.axis_index("rup")
    ids = jnp.where(mine, ids, 0).astype(jnp.bfloat16)
    ids = jnp.broadcast_to(ids.reshape(1, 1, points), (1, entries, points))
    moment = jnp.transpose(moment_tensor, (2, 1, 0, 3)).reshape(comps, entries, points)
    moment = jnp.concatenate([moment, ids])
    moment = jnp.broadcast_to(moment[None], (sects,) + moment.shape)
    moment, green_tensor, slip_rate = lax.optimization_barrier((moment, green_tensor, slip_rate))
    moment = lax.all_to_all(moment, "sect", split_axis=0, concat_axis=0, tiled=True)

    green, *parts = split(
        green_tensor.reshape(blocks * 2, comps, dirs, sects, sub, points),
        slip_rate.reshape(rup_rows, list_cols, 2, rups * sects, sub, points),
        PARTS,
    )
    green, moment, *parts = lax.optimization_barrier((green, moment, *parts))
    moment = lax.all_gather(moment, "rup", axis=0)
    green = lax.all_to_all(green, "sect", split_axis=0, concat_axis=0, tiled=True)

    fold = fold_table(cols, blocks, sub)
    rup = lax.axis_index("rup")
    spectrum = None
    first = 0
    before = green
    for i, part in enumerate(parts):
        if i == 0:
            part, before, moment = lax.optimization_barrier((part, before, moment))
        else:
            part, before = lax.optimization_barrier((part, before))
        arrived = part.reshape((sects * rups,) + part.shape[2:])
        arrived = lax.all_to_all(arrived, both, split_axis=0, concat_axis=0, tiled=True)
        if i == 0:
            green = before
        else:
            spectrum = contract(before, moment, green, fold, spectrum, done, width, blocks)
        done = first
        before = arrived.reshape(part.shape)
        first += part.shape[2]
    send = contract(before, moment, green, fold, spectrum, done, width, blocks)
    rup, send = lax.optimization_barrier((rup, send))
    high, low = transform_table(rup, 2 * frequencies // rups, frequencies, sects, rups, sub)

    all_freqs = lax.all_to_all(send, both, split_axis=0, concat_axis=0, tiled=True)
    return jnp.swapaxes(transform(all_freqs, high, low, dirs, sub), 0, 1)


def solution(mesh):
    placed = (
        P("sect", None, None, None, "rup", None),
        P("rup", "sect", None, None, None),
        P("rup", "sect", None, None),
        P("rup", "sect"),
        P("rup", "sect"),
    )
    return jax.shard_map(
        body, mesh=mesh, in_specs=placed, out_specs=P("sect", None, "rup"), check_vma=False
    )
```

```python
import functools
import math

import jax
import jax.numpy as jnp
import numpy as np
from jax import lax
from jax.experimental import pallas as pl
from jax.experimental.pallas import tpu as pltpu
from jax.sharding import PartitionSpec as P

PARTS = (6, 2)
LANES = 128
PAD = 1


def load_rows(block_ref, wide_ref):
    rows = block_ref.shape[0]
    apart = wide_ref.shape[0] // rows
    for r in range(rows):
        block = block_ref[r].astype(jnp.float32).reshape(-1, block_ref.shape[-1])
        wide_ref[pl.ds(r * apart, block.shape[0])] = block
    return rows, apart


def split_kernel(count, *refs):
    green_ref, slip_ref, green_out = refs[:3]
    slip_outs = refs[3 : 3 + count]
    green_in, slip_in, green_stage = refs[3 + count : 6 + count]
    slip_stages = refs[6 + count : 6 + 2 * count]
    green_wide, slip_wide, green_got, green_sent, slip_got, slip_sent = refs[6 + 2 * count :]
    comps, _, dirs, sects, sub, _ = green_in.shape
    rups, _, lists, parts = slip_in.shape[:4]

    def green_load(c):
        return pltpu.make_async_copy(green_ref.at[:, c], green_in.at[c], green_got.at[c])

    def slip_load(k):
        piece = slip_ref.at[:, :, :, pl.ds(k * sects, sects)]
        return pltpu.make_async_copy(piece, slip_in.at[k], slip_got.at[k])

    def green_store():
        return pltpu.make_async_copy(green_stage, green_out, green_sent)

    def slip_store(i, k):
        return pltpu.make_async_copy(slip_stages[i].at[:, k], slip_outs[i].at[:, k], slip_sent.at[i, k])

    for c in range(comps):
        green_load(c).start()
    for k in range(rups):
        slip_load(k).start()

    def green_step(c, carry):
        green_load(c).wait()
        rows, apart = load_rows(green_in.at[c], green_wide)
        for s in range(sects):
            for f in range(sub):
                places = [(j * sects + s) * sub + f for j in range(dirs)]
                turned = [green_wide[pl.ds(place, rows, stride=apart)] for place in places]
                green_stage[s, f, c] = jnp.concatenate(turned, axis=0).astype(green_stage.dtype)
        return carry

    lax.fori_loop(0, comps, green_step, 0)
    green_store().start()

    def slip_step(k, carry):
        slip_load(k).wait()
        rows, apart = load_rows(slip_in.at[k], slip_wide)
        for part in range(parts):
            for d in range(sects):
                f = 0
                for stage in slip_stages:
                    for i in range(stage.shape[2]):
                        places = [((l * parts + part) * sects + d) * sub + f for l in range(lists)]
                        turned = [slip_wide[pl.ds(place, rows, stride=apart)] for place in places]
                        stage[d, k, i, part] = jnp.concatenate(turned, axis=0).astype(stage.dtype)
                        f += 1
        for i in range(count):
            slip_store(i, k).start()
        return carry

    lax.fori_loop(0, rups, slip_step, 0)
    green_store().wait()
    for k in range(rups):
        for i in range(count):
            slip_store(i, k).wait()


def split(green, slip, counts):
    green_rows, comps, dirs, sects, sub, points = green.shape
    rows, lists, parts, devices = slip.shape[:4]
    rups = devices // sects
    green_shape = (sects, sub, comps, dirs * green_rows, points)
    slip_shapes = [(sects, rups, count, parts, lists * rows, points) for count in counts]
    kind = green.dtype
    anywhere = pl.BlockSpec(memory_space=pl.ANY)
    return pl.pallas_call(
        functools.partial(split_kernel, len(counts)),
        in_specs=[anywhere, anywhere],
        out_specs=[anywhere] * (1 + len(counts)),
        out_shape=[jax.ShapeDtypeStruct(shape, kind) for shape in [green_shape] + slip_shapes],
        scratch_shapes=[
            pltpu.VMEM((comps, green_rows, dirs, sects, sub, points), kind),
            pltpu.VMEM((rups, rows, lists, parts, sects, sub, points), kind),
            *[pltpu.VMEM(shape, kind) for shape in [green_shape] + slip_shapes],
            pltpu.VMEM((green_rows * (dirs * sects * sub + PAD), points), jnp.float32),
            pltpu.VMEM((rows * (lists * parts * sects * sub + PAD), points), jnp.float32),
            pltpu.SemaphoreType.DMA((comps,)),
            pltpu.SemaphoreType.DMA,
            pltpu.SemaphoreType.DMA((rups,)),
            pltpu.SemaphoreType.DMA((len(counts), rups)),
        ],
        compiler_params=pltpu.CompilerParams(vmem_limit_bytes=67_000_000),
        cost_estimate=pl.CostEstimate(
            flops=2 * (green.size + slip.size), bytes_accessed=4 * (green.size + slip.size), transcendentals=0
        ),
    )(green, slip)


def contract_kernel(width, blocks, sub, first, final, *refs):
    if final:
        slip_ref, moment_ref, green_ref, fold_ref, prev_ref, out_ref, sum_ref = refs
    else:
        slip_ref, moment_ref, green_ref, fold_ref, sum_ref = refs
    rups, sects, rows_per = moment_ref.shape[:3]
    comps = rows_per - 1
    entries, points = moment_ref.shape[3:]
    cols = sects * width
    green = jnp.concatenate([green_ref[:, 0, c].reshape(cols, points) for c in range(comps)], axis=1)
    row = lax.broadcasted_iota(jnp.int32, (cols, LANES), 0)
    row_block = (row // width * blocks + row % (2 * blocks) // 2).astype(jnp.float32)
    ids = moment_ref[0, :, comps].astype(jnp.float32)
    for k in range(1, rups):
        ids = ids + moment_ref[k, :, comps].astype(jnp.float32)
    f = pl.program_id(0)

    @pl.when(f == 0)
    def _():
        sum_ref[...] = prev_ref[...] if final else jnp.zeros(sum_ref.shape, jnp.float32)

    spectrum = None
    for part in range(2):
        slip = slip_ref[:, :, 0, part]
        weighted = jnp.concatenate(
            [
                (slip * jnp.swapaxes(moment_ref[:, :, c], 0, 1)).reshape(sects * LANES, points)
                for c in range(comps)
            ],
            axis=1,
        )
        products = lax.dot_general(green, weighted, (((1,), (1,)), ((), ())), preferred_element_type=jnp.float32)
        rest = None
        for s in range(sects):
            kept = jnp.where(row_block == ids[s, :1], products[:, s * LANES : (s + 1) * LANES], 0.0)
            rest = kept if rest is None else rest + kept
        for _ in range(3):
            piece = rest.astype(jnp.bfloat16)
            term = jnp.dot(fold_ref[part], piece, preferred_element_type=jnp.float32)
            spectrum = term if spectrum is None else spectrum + term
            rest = rest - piece.astype(jnp.float32)
    sum_ref[: spectrum.shape[0]] += pltpu.roll(spectrum, f + first, 0)
    if final:

        @pl.when(f == pl.num_programs(0) - 1)
        def _():
            pairs = out_ref.shape[1]
            owned = 2 * pairs
            turned = sum_ref[...].T.reshape(rups, 2, entries // 2, LANES)
            turned = (turned[:, 0] + turned[:, 1]).reshape(rups * entries // 2, LANES)
            moved = pltpu.roll(turned, LANES // 2, 1)
            for s in range(sects):
                mine = turned[s * owned : s * owned + pairs] + moved[s * owned + pairs : (s + 1) * owned]
                for k in range(rups):
                    out_ref[s * rups + k] = mine


def contract(slip, moment, green, fold, prev, first, width, blocks):
    sects, rups, freqs, _, entries, points = slip.shape
    sub = green.shape[1]
    cols = sects * width
    ruptures = rups * entries // 2
    comps = moment.shape[2] - 1
    final = prev is not None
    in_specs = [
        pl.BlockSpec((sects, rups, 1, 2, entries, points), lambda f: (0, 0, f, 0, 0, 0)),
        pl.BlockSpec(moment.shape, lambda f: (0, 0, 0, 0, 0)),
        pl.BlockSpec((sects, 1) + green.shape[2:], lambda f: (0, f + first, 0, 0, 0)),
        pl.BlockSpec(fold.shape, lambda f: (0, 0, 0)),
    ]
    args = [slip, moment, green, fold]
    scratch = []
    if final:
        in_specs.append(pl.BlockSpec(prev.shape, lambda f: (0, 0)))
        args.append(prev)
        shape = (sects * rups, ruptures // sects // 2, LANES)
        scratch.append(pltpu.VMEM((LANES, LANES), jnp.float32))
    else:
        shape = (LANES, LANES)
    return pl.pallas_call(
        functools.partial(contract_kernel, width, blocks, sub, first, final),
        grid=(freqs,),
        in_specs=in_specs,
        out_specs=pl.BlockSpec(shape, lambda f: (0,) * len(shape)),
        out_shape=jax.ShapeDtypeStruct(shape, jnp.float32),
        scratch_shapes=scratch,
        compiler_params=pltpu.CompilerParams(vmem_limit_bytes=67_000_000),
        cost_estimate=pl.CostEstimate(
            flops=freqs * 4 * sects * rups * entries * comps * points * cols,
            bytes_accessed=freqs * (sects * rups * entries * points * 4 + comps * cols * points * 2),
            transcendentals=0,
        ),
    )(*args)


def fold_table(cols, blocks, sub):
    col = np.arange(cols)
    part, direction = col % 2, col // (2 * blocks) % 3
    out = np.arange(6 * sub)
    value = np.where(out % sub == 0, out // sub, -1)
    same = (direction[None, :] == (value % 3)[:, None]) & (value >= 0)[:, None]
    equal = part[None, :] == (value // 3)[:, None]
    sign = np.where(value // 3 == 0, -1.0, 1.0)[:, None]
    real_slip = np.where(same & equal, 1.0, 0.0)
    imag_slip = np.where(same & ~equal, sign, 0.0)
    return jnp.asarray(np.stack([real_slip, imag_slip]), jnp.bfloat16)


def transform_table(rup, times, frequencies, sects, rups, sub):
    samples = 2 * frequencies
    unit = 2.0 * math.pi / samples
    base = np.arange(sects)[:, None] * sub + np.arange(rups)[None, :] * (frequencies // rups)
    base = base.reshape(-1, 1) * np.arange(times)[None, :] % samples * unit
    rest = np.arange(sub)[None, :, None] * np.arange(samples).reshape(rups, 1, times) % samples * unit
    scale = 1.0 / math.sqrt(frequencies)
    base_cos, base_sin = (jnp.asarray(f(base) * scale, jnp.float32) for f in (np.cos, np.sin))
    rest_cos, rest_sin = (
        lax.dynamic_index_in_dim(jnp.asarray(f(rest), jnp.float32), rup, 0, keepdims=False) for f in (np.cos, np.sin)
    )
    cosine = rest_cos[:, None] * base_cos[None] - rest_sin[:, None] * base_sin[None]
    sine = rest_sin[:, None] * base_cos[None] + rest_cos[:, None] * base_sin[None]
    table = jnp.stack([cosine, -sine]).reshape(2 * frequencies, times)
    high = lax.reduce_precision(table, 8, 7)
    return high.astype(jnp.bfloat16), (table - high).astype(jnp.bfloat16)


def transform_kernel(sub, spectra_ref, high_ref, low_ref, out_ref, turned_ref, left_ref):
    dirs, owned = out_ref.shape[:2]
    devices = spectra_ref.shape[0]
    used = 2 * dirs * sub
    rows = left_ref.shape[0]
    pairs = owned // 2
    for r in range(pairs):
        turned = spectra_ref[:, r, :].T
        turned_ref[r] = turned[:used]
        turned_ref[r + pairs] = turned[LANES // 2 : LANES // 2 + used]
    left_ref[...] = jnp.zeros(left_ref.shape, jnp.float32)
    for part in range(2):
        for f in range(sub):
            place = pl.ds((part * sub + f) * devices, devices)
            for r in range(owned):
                for j in range(dirs):
                    row = (part * dirs + j) * sub + f
                    left_ref[pl.ds(j * owned + r, 1), place] = turned_ref[r, pl.ds(row, 1), :]
    left = left_ref[...]
    high = left.astype(jnp.bfloat16)
    low = (left - high.astype(jnp.float32)).astype(jnp.bfloat16)
    both = jnp.concatenate([high, low], axis=0)
    first = jnp.dot(both, high_ref[...], preferred_element_type=jnp.float32)
    second = jnp.dot(high, low_ref[...], preferred_element_type=jnp.float32)
    result = first[:rows] + (first[rows:] + second)
    for j in range(dirs):
        out_ref[j] = result[j * owned : (j + 1) * owned]


def transform(spectra, high, low, dirs, sub):
    devices, pairs, _ = spectra.shape
    owned = 2 * pairs
    depth, times = high.shape
    return pl.pallas_call(
        functools.partial(transform_kernel, sub),
        out_shape=jax.ShapeDtypeStruct((dirs, owned, times), jnp.float32),
        scratch_shapes=[
            pltpu.VMEM((owned, 2 * dirs * sub, devices), jnp.float32),
            pltpu.VMEM((16, depth), jnp.float32),
        ],
        compiler_params=pltpu.CompilerParams(vmem_limit_bytes=16 * 2**20),
    )(spectra, high, low)


def body(green_tensor, slip_rate, moment_tensor, section_ids, block_ids):
    sects = lax.axis_size("sect")
    rups = lax.axis_size("rup")
    both = ("sect", "rup")
    blocks, _, comps, dirs, freq_slice, points = green_tensor.shape
    rup_rows, list_cols = section_ids.shape
    entries = rup_rows * list_cols
    frequencies = slip_rate.shape[3]
    sub = freq_slice // sects
    width = 2 * dirs * blocks
    cols = sects * width

    ids = jnp.tile((section_ids * blocks + block_ids).T.reshape(entries), rups)
    mine = jnp.arange(points, dtype=jnp.int32) // entries == lax.axis_index("rup")
    ids = jnp.where(mine, ids, 0).astype(jnp.bfloat16)
    ids = jnp.broadcast_to(ids.reshape(1, 1, points), (1, entries, points))
    moment = jnp.transpose(moment_tensor, (2, 1, 0, 3)).reshape(comps, entries, points)
    moment = jnp.concatenate([moment, ids])
    moment = jnp.broadcast_to(moment[None], (sects,) + moment.shape)
    moment, green_tensor, slip_rate = lax.optimization_barrier((moment, green_tensor, slip_rate))
    moment = lax.all_to_all(moment, "sect", split_axis=0, concat_axis=0, tiled=True)

    green, *parts = split(
        green_tensor.reshape(blocks * 2, comps, dirs, sects, sub, points),
        slip_rate.reshape(rup_rows, list_cols, 2, rups * sects, sub, points),
        PARTS,
    )
    green, moment, *parts = lax.optimization_barrier((green, moment, *parts))
    moment = lax.all_gather(moment, "rup", axis=0)
    green = lax.all_to_all(green, "sect", split_axis=0, concat_axis=0, tiled=True)

    fold = fold_table(cols, blocks, sub)
    rup = lax.axis_index("rup")
    spectrum = None
    first = 0
    before = green
    for i, part in enumerate(parts):
        if i == 0:
            part, before, moment = lax.optimization_barrier((part, before, moment))
        else:
            part, before = lax.optimization_barrier((part, before))
        arrived = part.reshape((sects * rups,) + part.shape[2:])
        arrived = lax.all_to_all(arrived, both, split_axis=0, concat_axis=0, tiled=True)
        if i == 0:
            green = before
        else:
            spectrum = contract(before, moment, green, fold, spectrum, done, width, blocks)
        done = first
        before = arrived.reshape(part.shape)
        first += part.shape[2]
    send = contract(before, moment, green, fold, spectrum, done, width, blocks)
    rup, send = lax.optimization_barrier((rup, send))
    high, low = transform_table(rup, 2 * frequencies // rups, frequencies, sects, rups, sub)

    all_freqs = lax.all_to_all(send, both, split_axis=0, concat_axis=0, tiled=True)
    return jnp.swapaxes(transform(all_freqs, high, low, dirs, sub), 0, 1)


def solution(mesh):
    placed = (
        P("sect", None, None, None, "rup", None),
        P("rup", "sect", None, None, None),
        P("rup", "sect", None, None),
        P("rup", "sect"),
        P("rup", "sect"),
    )
    return jax.shard_map(
        body, mesh=mesh, in_specs=placed, out_specs=P("sect", None, "rup"), check_vma=False
    )
```
